256 devices in a mesh: blk: 64 (over z, x_hi, y), rep: 4 (over x_lo, core).
Axes of the slice: x: 4 (x_hi: 2, x_lo: 2; x = x_hi * 2 + x_lo), y: 4, z: 8, core: 2. Of those that a mesh axis runs over, the one named last changes fastest.
Arguments:
- node_feats: bfloat16 [65536, 256], P(('blk', 'rep')), may hold values from -6 to 6
- tile_vals: bfloat16 [64, 4, 128, 128, 128], P('blk', 'rep'), may hold values from -0.0625 to 0.0625
- tile_row: int32 [64, 4, 128], P('blk', 'rep'), may hold values from 0 to 7
- tile_col: int32 [64, 4, 128], P('blk', 'rep'), may hold values from 0 to 127, as said below
- tile_count: int32 [64, 4], P('blk', 'rep'), may hold values from 16 to 128, as said below
- w_agg: bfloat16 [256, 256], replicated, may hold values from -0.375 to 0.375
- w_self: bfloat16 [256, 256], replicated, may hold values from -0.375 to 0.375
- bias: float32 [256], replicated, may hold values from -1 to 1
- cotangent: bfloat16 [65536, 256], P(('blk', 'rep')), may hold values from -6 to 6
Outputs:
- updated: bfloat16 [65536, 256], P(('blk', 'rep'))
- feat_grad: bfloat16 [65536, 256], P(('blk', 'rep'))
- tile_grads: bfloat16 [64, 4, 128, 128, 128], P('blk', 'rep')
- weight_grads: float32 [2, 256, 256], replicated
The draws below stay inside these ranges and needn't reach their ends.
Inputs may be any that keep to these rules, and one draw needn't show every extreme that they name: `tile_col`: each slot names a column tile of a row group at most 2 cycle steps away or a power of two steps away around the closed cycle of 64 groups. `tile_count`: one of 128, 64, 32 or 16; some (g, r) has exactly 128.
All inputs are finite; a program needn't handle non-finite values.
Results may differ from the reference program's by a relative error of at most 0.0059.
Values may be sent and summed in bfloat16 or wider, within the bound.
No kernel may reach another device: no remote copies, remote signals or barrier semaphores. Data moves between devices by JAX's collectives and lax.ppermute only.
A program may use at most 128 MiB of HBM per device.

```python
import math
import jax
import jax.numpy as jnp
from jax import lax

D = 256
TILE = 128
ROWT = 2
KT_RT = 16
GROUPS = 64
REPS = 4
KT = 128
NODES = 65536
N_REP = 4


def draw_tile_col(key, part):
    key = jax.random.fold_in(key, 11)
    key_near, key_power, key_sign, key_pick, key_sub = jax.random.split(key, 5)
    shape = (GROUPS, REPS, KT)
    group_ids = jnp.arange(GROUPS, dtype=jnp.int32)[:, None, None]
    near_off = jax.random.randint(key_near, shape, -2, 3, dtype=jnp.int32)
    levels = max(GROUPS.bit_length() - 1, 1)
    power = jax.random.randint(key_power, shape, 0, levels, dtype=jnp.int32)
    far_off = jnp.left_shift(jnp.ones(shape, jnp.int32), power)
    sign_pick = jax.random.randint(key_sign, shape, 0, 2, dtype=jnp.int32) * 2 - 1
    which_one = jax.random.randint(key_pick, shape, 0, 2, dtype=jnp.int32)
    offset = jnp.where(which_one == 0, near_off, sign_pick * far_off)
    owner = (group_ids + offset) % GROUPS
    sub_tile = jax.random.randint(key_sub, shape, 0, ROWT, dtype=jnp.int32)
    return (owner * ROWT + sub_tile).astype(jnp.int32)


def draw_tile_count(key, part):
    key = jax.random.fold_in(key, 7)
    key_level, key_full = jax.random.split(key, 2)
    level = jax.random.randint(key_level, (GROUPS * REPS,), 0, 4, dtype=jnp.int32)
    counts = jnp.right_shift(jnp.full((GROUPS * REPS,), KT, jnp.int32), level)
    full_at = jax.random.randint(key_full, (), 0, GROUPS * REPS, dtype=jnp.int32)
    counts = counts.at[full_at].set(KT)
    return counts.reshape(GROUPS, REPS).astype(jnp.int32)


def place_ends(array, stream_key, least, top_value):
    spot = [jax.random.randint(jax.random.fold_in(stream_key, axis), (), 0, length) for axis, length in enumerate(array.shape)]
    widest = array.shape.index(max(array.shape))
    next_to = spot[:widest] + [(spot[widest] + 1) % array.shape[widest]] + spot[widest + 1:]
    return array.at[tuple(spot)].set(least).at[tuple(next_to)].set(top_value)


def block_levels(key, extent, pieces, low, high):
    factor_of, own = 1.0, jax.random.fold_in(key, 6)
    for axis_at, blocks in pieces:
        draws = jnp.exp(jax.random.uniform(jax.random.fold_in(own, axis_at), (blocks,), jnp.float32, low / len(pieces), high / len(pieces)))
        factor_of = factor_of * jnp.repeat(draws, extent[axis_at] // blocks).reshape([-1 if axis == axis_at else 1 for axis in range(len(extent))])
    return factor_of


def scatter_about(stream_key, shape, scale, most, cuts=(), held_as=jnp.bfloat16):
    array = scale * jax.random.normal(stream_key, shape, jnp.float32)
    if cuts:
        array = array * block_levels(stream_key, shape, cuts, -0.22, 0.18)
    return jnp.clip(array, -most, most).astype(held_as)


def setup_inputs(seed: int = 0) -> dict:
    arg_keys = jax.random.split(jax.random.key(seed), 10)
    return {
        "node_feats": scatter_about(arg_keys[0], (NODES, D), 1.0, 6.0, ((0, 256),)),
        "tile_vals": scatter_about(arg_keys[1], (GROUPS, REPS, KT, TILE, TILE), (KT_RT * N_REP * TILE) ** -0.5, 0.0625, ((0, 64), (1, 4))),
        "tile_row": place_ends(jax.random.randint(arg_keys[2], (GROUPS, REPS, KT), 0, REPS * ROWT), jax.random.fold_in(arg_keys[2], 1), 0, (REPS * ROWT) - 1).astype(jnp.int32),
        "tile_col": draw_tile_col(jax.random.fold_in(arg_keys[9], 71), 0),
        "tile_count": draw_tile_count(jax.random.fold_in(arg_keys[9], 71), 0),
        "w_agg": scatter_about(arg_keys[5], (D, D), D ** -0.5, 0.375),
        "w_self": scatter_about(arg_keys[6], (D, D), D ** -0.5, 0.375),
        "bias": jnp.clip(jax.random.uniform(arg_keys[7], (D,), jnp.float32, -1.0, 1.0), -1.0, 1.0),
        "cotangent": scatter_about(arg_keys[8], (NODES, D), 1.0, 6.0, ((0, 256),)),
    }


def pick_blocks(block_set, indices):
    return block_set[indices]

def reference(node_feats, tile_vals, tile_row, tile_col, tile_count, w_agg, w_self, bias, cotangent):
    high = lax.Precision.HIGHEST
    row_tiles = REPS * ROWT
    col_tiles = GROUPS * ROWT
    blocks = node_feats.reshape(GROUPS, REPS, ROWT, TILE, D)
    col_sets = jnp.transpose(blocks, (1, 0, 2, 3, 4)).reshape(REPS, col_tiles, TILE, D)
    live_mask = (jnp.arange(KT, dtype=jnp.int32)[None, None, :] < tile_count[:, :, None]).astype(jnp.float32)

    def forward_group(group):
        values = tile_vals[group].astype(jnp.float32)
        columns = jax.vmap(pick_blocks)(col_sets, tile_col[group]).astype(jnp.float32)
        products = jnp.einsum('rkij,rkjd->rkid', values, columns, precision=high)
        row_hot = (tile_row[group][:, :, None] == jnp.arange(row_tiles, dtype=jnp.int32)).astype(jnp.float32)
        row_hot = row_hot * live_mask[group][:, :, None]
        return jnp.einsum('rkq,rkid->qid', row_hot, products, precision=high)
    aggregate = lax.map(forward_group, jnp.arange(GROUPS, dtype=jnp.int32)).reshape(NODES, D)
    agg_b = aggregate.astype(jnp.bfloat16)
    preact = jnp.dot(agg_b, w_agg, preferred_element_type=jnp.float32) + jnp.dot(node_feats, w_self, preferred_element_type=jnp.float32) + bias
    updated = (node_feats.astype(jnp.float32) + jax.nn.silu(preact)).astype(jnp.bfloat16)
    sigmoid_pre = jax.nn.sigmoid(preact)
    silu_slope = sigmoid_pre * (1.0 + preact * (1.0 - sigmoid_pre))
    dpre = (cotangent.astype(jnp.float32) * silu_slope).astype(jnp.bfloat16)
    grad_scale = 1.0 / math.sqrt(NODES)
    grad_agg = jnp.dot(agg_b.T, dpre, preferred_element_type=jnp.float32) * grad_scale
    grad_self = jnp.dot(node_feats.T, dpre, preferred_element_type=jnp.float32) * grad_scale
    weight_grads = jnp.stack([grad_agg, grad_self])
    dagg = jnp.dot(dpre, w_agg.T, preferred_element_type=jnp.float32).astype(jnp.bfloat16)
    row_sets = dagg.reshape(GROUPS, row_tiles, TILE, D)
    tile_scale = 1.0 / math.sqrt(D)

    def backward_group(carried, group):
        values = tile_vals[group].astype(jnp.float32)
        columns = jax.vmap(pick_blocks)(col_sets, tile_col[group]).astype(jnp.float32)
        row_blocks = row_sets[group][tile_row[group]].astype(jnp.float32)
        mask_now = live_mask[group]
        grads_now = jnp.einsum('rkid,rkjd->rkij', row_blocks, columns, precision=high)
        grads_now = (grads_now * (mask_now * tile_scale)[:, :, None, None]).astype(jnp.bfloat16)
        contrib = jnp.einsum('rkij,rkid->rkjd', values, row_blocks, precision=high)
        col_hot = (tile_col[group][:, :, None] == jnp.arange(col_tiles, dtype=jnp.int32)).astype(jnp.float32)
        col_hot = col_hot * mask_now[:, :, None]
        carried = carried + jnp.einsum('rkc,rkjd->rcjd', col_hot, contrib, precision=high)
        return (carried, grads_now)
    start_sum = jnp.zeros((REPS, col_tiles, TILE, D), jnp.float32)
    col_sum, tile_grads = lax.scan(backward_group, start_sum, jnp.arange(GROUPS, dtype=jnp.int32))
    backward = jnp.transpose(col_sum.reshape(REPS, GROUPS, ROWT, TILE, D), (1, 0, 2, 3, 4)).reshape(NODES, D)
    feat_grad = cotangent.astype(jnp.float32) + jnp.dot(dpre, w_self.T, preferred_element_type=jnp.float32) + backward
    return (updated, feat_grad.astype(jnp.bfloat16), tile_grads, weight_grads)
```

```python
import math

import jax
import jax.numpy as jnp
from jax import lax
from jax.experimental import pallas as pl
from jax.experimental.pallas import tpu as pltpu
from jax.sharding import PartitionSpec as P

DISTANCES = (0, 1, 2, 4, 8, 16, 32, 48, 56, 60, 62, 63)
VMEM = pl.BlockSpec(memory_space=pltpu.VMEM)
SMEM = pl.BlockSpec(memory_space=pltpu.SMEM)
ANY = pl.BlockSpec(memory_space=pl.ANY)
LIMIT = 40 * 1024 * 1024


def params():
    return pltpu.CompilerParams(vmem_limit_bytes=LIMIT)


def dot_nt(a, b):
    return lax.dot_general(a, b, (((1,), (1,)), ((), ())), preferred_element_type=jnp.float32)


def dot_tn(a, b):
    return lax.dot_general(a, b, (((0,), (0,)), ((), ())), preferred_element_type=jnp.float32)


def build_kernel(row_ref, loc_ref, count_ref, vals_ref, dense_ref, acc_ref):
    col_tiles = dense_ref.shape[1] // 128
    row_tiles = dense_ref.shape[0] // 128

    def clear(i, c):
        acc_ref[i] = jnp.zeros((128, 128), jnp.float32)
        return c

    lax.fori_loop(0, row_tiles * col_tiles, clear, 0)

    def add(k, c):
        at = row_ref[k] * col_tiles + loc_ref[k]
        acc_ref[at] = acc_ref[at] + vals_ref[k].astype(jnp.float32)
        return c

    lax.fori_loop(0, count_ref[0], add, 0)

    def cast(q, c):
        rows = pl.ds(pl.multiple_of(q * 128, 128), 128)
        for t in range(col_tiles):
            dense_ref[rows, t * 128 : (t + 1) * 128] = acc_ref[q * col_tiles + t].astype(jnp.bfloat16)
        return c

    lax.fori_loop(0, row_tiles, cast, 0)


def load_blocks(rep, dense_ref, buf, sems):
    copies = []
    for k in range(4):
        rows = pl.ds(pl.multiple_of((rep ^ k) * 256, 256), 256)
        copies.append(pltpu.make_async_copy(dense_ref.at[rows], buf.at[k], sems.at[k]))
    for copy in copies:
        copy.start()
    return copies


def forward_kernel(rep_ref, dense_ref, *refs):
    feats, outs, (buf, sems) = refs[:12], refs[12:16], refs[16:]
    copies = load_blocks(rep_ref[0], dense_ref, buf, sems)
    for k in (3, 2, 1, 0):
        copies[k].wait()
        total = jnp.zeros((256, 256), jnp.float32)
        for o in range(12):
            total = total + jnp.dot(
                buf[k, :, o * 256 : (o + 1) * 256], feats[o][...], preferred_element_type=jnp.float32
            )
        outs[k][...] = total.astype(outs[k].dtype)


def update_kernel(p0, p1, p2, p3, x_ref, cot_ref, wa_ref, ws_ref, b_ref, upd_ref, dagg_ref, base_ref, grads_ref):
    agg = p0[...] + p1[...].astype(jnp.float32) + p2[...].astype(jnp.float32) + p3[...].astype(jnp.float32)
    agg_b = agg.astype(jnp.bfloat16)
    x = x_ref[...]
    pre = (
        jnp.dot(agg_b, wa_ref[...], preferred_element_type=jnp.float32)
        + jnp.dot(x, ws_ref[...], preferred_element_type=jnp.float32)
        + b_ref[...]
    )
    s = 1.0 / (1.0 + jnp.exp(-pre))
    upd_ref[...] = (x.astype(jnp.float32) + pre * s).astype(jnp.bfloat16)
    cot = cot_ref[...].astype(jnp.float32)
    dpre = (cot * (s * (1.0 + pre * (1.0 - s)))).astype(jnp.bfloat16)
    dagg_ref[...] = dot_nt(dpre, wa_ref[...]).astype(jnp.bfloat16)
    base_ref[...] = cot + dot_nt(dpre, ws_ref[...])
    scale = 1.0 / 256.0
    for i, a in enumerate((agg_b, x)):
        total = dot_tn(a, dpre) * scale
        grads_ref[2 * i] = total[:, :128]
        grads_ref[2 * i + 1] = total[:, 128:]


def scatter_kernel(rep_ref, dense_ref, d0, d1, d2, d3, *refs):
    outs, (buf, sems) = refs[:12], refs[12:]
    copies = load_blocks(rep_ref[0], dense_ref, buf, sems)
    turned = [d[...].T for d in (d0, d1, d2, d3)]
    for copy in copies:
        copy.wait()
    for o in range(12):
        total = jnp.zeros((256, 256), jnp.float32)
        for k in range(4):
            total = total + jnp.dot(
                turned[k], buf[k, :, o * 256 : (o + 1) * 256], preferred_element_type=jnp.float32
            )
        outs[o][...] = total.astype(outs[o].dtype)


def tile_grads_kernel(rep_ref, row_ref, loc_ref, count_ref, d0, d1, d2, d3, *refs):
    feats, out_ref, (grid_ref, zero_ref, sem) = refs[:12], refs[12], refs[13:]
    daggs = (d0, d1, d2, d3)
    rep = rep_ref[0]
    zero_ref[...] = jnp.zeros_like(zero_ref)
    slots = out_ref.shape[0]
    for k in range(4):
        first = (rep ^ k) * 2
        for o in range(12):
            block = (dot_nt(daggs[k][...], feats[o][...]) * (1.0 / 16.0)).astype(jnp.bfloat16)
            for a in range(2):
                for b in range(2):
                    grid_ref[(first + a) * 24 + 2 * o + b] = block[
                        a * 128 : (a + 1) * 128, b * 128 : (b + 1) * 128
                    ]

    def send(k, c):
        pltpu.make_async_copy(grid_ref.at[row_ref[k] * 24 + loc_ref[k]], out_ref.at[k], sem).start()
        return c

    def blank(k, c):
        pltpu.make_async_copy(zero_ref, out_ref.at[k], sem).start()
        return c

    lax.fori_loop(0, count_ref[0], send, 0)
    lax.fori_loop(count_ref[0], slots, blank, 0)

    def wait(k, c):
        pltpu.make_async_copy(zero_ref, out_ref.at[k], sem).wait()
        return c

    lax.fori_loop(0, slots, wait, 0)


def finish_kernel(base_ref, own_ref, *refs):
    terms, out_ref = refs[:-1], refs[-1]
    total = own_ref[...]
    for t in terms:
        total = total + t[...].astype(jnp.float32)
    out_ref[...] = (base_ref[...] + total.T).astype(jnp.bfloat16)


def local(node_feats, tile_vals, tile_row, tile_col, tile_count, w_agg, w_self, bias, cotangent):
    n_blk = lax.axis_size("blk")
    group = lax.axis_index("blk")
    rep = lax.axis_index("rep").reshape(1).astype(jnp.int32)
    row = tile_row[0, 0]
    count = tile_count[0]
    away = (lax.div(tile_col[0, 0], 2) - group + n_blk) & (n_blk - 1)
    loc = lax.rem(tile_col[0, 0], 2)
    for d in DISTANCES[1:]:
        loc = loc + 2 * (away >= d).astype(jnp.int32)
    loc = loc.astype(jnp.int32)

    def shape(s, t=jnp.bfloat16):
        return jax.ShapeDtypeStruct(s, t)

    def from_blk(x, d):
        return lax.ppermute(x, "blk", [(i, (i - d) % n_blk) for i in range(n_blk)])

    def to_rep(x, k):
        return lax.ppermute(x, "rep", [(i, i ^ k) for i in range(4)])

    feats = [node_feats] + [from_blk(node_feats, d) for d in DISTANCES[1:]]
    dense = pl.pallas_call(
        build_kernel,
        out_shape=shape((1024, 3072)),
        in_specs=[SMEM, SMEM, SMEM, VMEM],
        out_specs=VMEM,
        scratch_shapes=[pltpu.VMEM((192, 128, 128), jnp.float32)],
        compiler_params=params(),
        cost_estimate=pl.CostEstimate(flops=0, bytes_accessed=10 << 20, transcendentals=0),
        name="build",
    )(row, loc, count, tile_vals[0, 0])

    block = (256, 256)
    blocks = [pltpu.VMEM((4, 256, 3072), jnp.bfloat16), pltpu.SemaphoreType.DMA((4,))]
    parts = pl.pallas_call(
        forward_kernel,
        out_shape=[shape(block, jnp.float32)] + [shape(block)] * 3,
        in_specs=[SMEM, ANY] + [VMEM] * 12,
        out_specs=[VMEM] * 4,
        scratch_shapes=blocks,
        compiler_params=params(),
        cost_estimate=pl.CostEstimate(flops=2 * 1024 * 3072 * 256, bytes_accessed=8 << 20, transcendentals=0),
        name="forward",
    )(rep, dense, *feats)
    swapped = [parts[0]] + [to_rep(parts[k], k) for k in (1, 2, 3)]

    updated, dagg, base, grads = pl.pallas_call(
        update_kernel,
        out_shape=[shape(block), shape(block), shape(block, jnp.float32), shape((4, 256, 128), jnp.float32)],
        in_specs=[VMEM] * 9,
        out_specs=[VMEM] * 4,
        compiler_params=params(),
        cost_estimate=pl.CostEstimate(flops=12 * 256**3, bytes_accessed=2 << 20, transcendentals=65536),
        name="update",
    )(*swapped, node_feats, cotangent, w_agg, w_self, bias.reshape(1, 256))

    daggs = [dagg] + [to_rep(dagg, k) for k in (1, 2, 3)]
    terms = pl.pallas_call(
        scatter_kernel,
        out_shape=[shape(block, jnp.float32)] + [shape(block)] * 11,
        in_specs=[SMEM, ANY] + [VMEM] * 4,
        out_specs=[VMEM] * 12,
        scratch_shapes=blocks,
        compiler_params=params(),
        cost_estimate=pl.CostEstimate(flops=2 * 1024 * 3072 * 256, bytes_accessed=8 << 20, transcendentals=0),
        name="scatter",
    )(rep, dense, *daggs)
    arrived = [from_blk(t, -d) for t, d in zip(terms[1:], DISTANCES[1:])]

    tile_grads = pl.pallas_call(
        tile_grads_kernel,
        out_shape=shape((128, 128, 128)),
        in_specs=[SMEM] * 4 + [VMEM] * 16,
        out_specs=ANY,
        scratch_shapes=[
            pltpu.VMEM((192, 128, 128), jnp.bfloat16),
            pltpu.VMEM((128, 128), jnp.bfloat16),
            pltpu.SemaphoreType.DMA,
        ],
        compiler_params=params(),
        cost_estimate=pl.CostEstimate(flops=2 * 1024 * 3072 * 256, bytes_accessed=8 << 20, transcendentals=0),
        name="tile_grads",
    )(rep, row, loc, count, *daggs, *feats)

    feat_grad = pl.pallas_call(
        finish_kernel,
        out_shape=shape(block),
        in_specs=[VMEM] * 13,
        out_specs=VMEM,
        compiler_params=params(),
        cost_estimate=pl.CostEstimate(flops=0, bytes_accessed=2 << 20, transcendentals=0),
        name="finish",
    )(base, *terms[:1], *arrived)

    quarter = jnp.sum(lax.all_to_all(grads, "rep", 0, 0, tiled=True), axis=0)
    piece = jnp.sum(lax.all_to_all(quarter.reshape(n_blk, 4, 128), "blk", 0, 0, tiled=True), axis=0)
    whole = lax.all_to_all(jnp.broadcast_to(piece[None], (n_blk, 4, 128)), "blk", 0, 0, tiled=True)
    quarters = lax.all_to_all(jnp.broadcast_to(whole.reshape(1, 256, 128), (4, 256, 128)), "rep", 0, 0, tiled=True)
    weight_grads = jnp.stack(
        [jnp.concatenate([quarters[2 * i], quarters[2 * i + 1]], axis=1) for i in range(2)]
    )
    return updated, feat_grad, tile_grads.reshape(1, 1, 128, 128, 128), weight_grads


def solution(mesh):
    in_specs = (
        P(("blk", "rep"), None),
        P("blk", "rep", None, None, None),
        P("blk", "rep", None),
        P("blk", "rep", None),
        P("blk", "rep"),
        P(),
        P(),
        P(),
        P(("blk", "rep"), None),
    )
    out_specs = (
        P(("blk", "rep"), None),
        P(("blk", "rep"), None),
        P("blk", "rep", None, None, None),
        P(),
    )
    return jax.shard_map(local, mesh=mesh, in_specs=in_specs, out_specs=out_specs, check_vma=False)
```

```python
import functools

import jax
import jax.numpy as jnp
from jax import lax
from jax.experimental import pallas as pl
from jax.experimental.pallas import tpu as pltpu
from jax.sharding import PartitionSpec as P

DISTANCES = (0, 1, 2, 4, 8, 16, 32, 48, 56, 60, 62, 63)
VMEM = pl.BlockSpec(memory_space=pltpu.VMEM)
SMEM = pl.BlockSpec(memory_space=pltpu.SMEM)
ANY = pl.BlockSpec(memory_space=pl.ANY)
HBM = pl.BlockSpec(memory_space=pltpu.HBM)


def dot_nt(a, b):
    return lax.dot_general(a, b, (((1,), (1,)), ((), ())), preferred_element_type=jnp.float32)


def dot_tn(a, b):
    return lax.dot_general(a, b, (((0,), (0,)), ((), ())), preferred_element_type=jnp.float32)


def build_kernel(row_ref, loc_ref, count_ref, vals_ref, dense_ref, acc_ref, held_ref, sems):
    parts = sems.shape[0]
    share = held_ref.shape[0] // parts
    copies = [
        pltpu.make_async_copy(
            vals_ref.at[pl.ds(p * share, share)], held_ref.at[pl.ds(p * share, share)], sems.at[p]
        )
        for p in range(parts)
    ]
    for copy in copies:
        copy.start()
    col_tiles = dense_ref.shape[1] // 128
    row_tiles = dense_ref.shape[0] // 128

    def clear(i, c):
        acc_ref[i] = jnp.zeros((128, 128), jnp.float32)
        return c

    lax.fori_loop(0, row_tiles * col_tiles, clear, 0)

    def add(k, c):
        at = row_ref[k] * col_tiles + loc_ref[k]
        acc_ref[at] = acc_ref[at] + held_ref[k].astype(jnp.float32)
        return c

    for p, copy in enumerate(copies):
        copy.wait()
        lax.fori_loop(p * share, jnp.minimum((p + 1) * share, count_ref[0]), add, 0)

    def cast(q, c):
        rows = pl.ds(pl.multiple_of(q * 128, 128), 128)
        for t in range(col_tiles):
            dense_ref[rows, t * 128 : (t + 1) * 128] = acc_ref[q * col_tiles + t].astype(jnp.bfloat16)
        return c

    lax.fori_loop(0, row_tiles, cast, 0)


def group_rows(rep, k):
    return pl.ds(pl.multiple_of((rep ^ k) * 256, 256), 256)


def forward_kernel(ks, rep_ref, dense_ref, *refs):
    feats, outs = refs[:12], refs[12:]
    for k, out in zip(ks, outs):
        total = jnp.zeros((256, 256), jnp.float32)
        for o in range(12):
            total = total + jnp.dot(
                dense_ref[group_rows(rep_ref[0], k), o * 256 : (o + 1) * 256],
                feats[o][...],
                preferred_element_type=jnp.float32,
            )
        out[...] = total.astype(out.dtype)


def update_kernel(
    rep_ref, own_ref, sib_ref, far_ref, x_ref, cot_ref, wa_ref, ws_ref, b_ref,
    upd_ref, dagg_ref, base_ref, g0_ref, g1_ref, g2_ref, g3_ref, grads_ref,
):
    agg = own_ref[...] + sib_ref[...].astype(jnp.float32) + far_ref[...].astype(jnp.float32)
    agg_b = agg.astype(jnp.bfloat16)
    x = x_ref[...]
    pre = (
        jnp.dot(agg_b, wa_ref[...], preferred_element_type=jnp.float32)
        + jnp.dot(x, ws_ref[...], preferred_element_type=jnp.float32)
        + b_ref[...]
    )
    s = 1.0 / (1.0 + jnp.exp(-pre))
    upd_ref[...] = (x.astype(jnp.float32) + pre * s).astype(jnp.bfloat16)
    cot = cot_ref[...].astype(jnp.float32)
    dpre = (cot * (s * (1.0 + pre * (1.0 - s)))).astype(jnp.bfloat16)
    dagg_ref[...] = dot_nt(dpre, wa_ref[...]).astype(jnp.bfloat16)
    base_ref[...] = cot + dot_nt(dpre, ws_ref[...])
    scale = 1.0 / 256.0
    for i, a in enumerate((agg_b, x)):
        total = dot_tn(a, dpre) * scale
        grads_ref[2 * i] = total[:, :128]
        grads_ref[2 * i + 1] = total[:, 128:]
    for k, out in enumerate((g0_ref, g1_ref, g2_ref, g3_ref)):
        out[...] = grads_ref[rep_ref[0] ^ k]


def scatter_kernel(rep_ref, dense_ref, d0, d1, d2, d3, *outs):
    turned = [d[...].T for d in (d0, d1, d2, d3)]
    for o in range(12):
        total = jnp.zeros((256, 256), jnp.float32)
        for k in range(4):
            total = total + jnp.dot(
                turned[k],
                dense_ref[group_rows(rep_ref[0], k), o * 256 : (o + 1) * 256],
                preferred_element_type=jnp.float32,
            )
        outs[o][...] = total.astype(outs[o].dtype)


def spread_kernel(pieces_ref, out_ref):
    total = jnp.sum(pieces_ref[...], axis=0)
    out_ref[...] = jnp.broadcast_to(total[None], out_ref.shape)


def join_kernel(rep_ref, q0, q1, q2, q3, out_ref, quarters_ref):
    for k, q in enumerate((q0, q1, q2, q3)):
        quarters_ref[rep_ref[0] ^ k] = q[...]
    for i in range(2):
        out_ref[i, :, :128] = quarters_ref[2 * i]
        out_ref[i, :, 128:] = quarters_ref[2 * i + 1]


def tile_grads_kernel(rep_ref, row_ref, loc_ref, count_ref, d0, d1, d2, d3, *refs):
    feats, out_ref, (grid_ref, zero_ref, sem) = refs[:12], refs[12], refs[13:]
    daggs = (d0, d1, d2, d3)
    rep = rep_ref[0]
    zero_ref[...] = jnp.zeros_like(zero_ref)
    slots = out_ref.shape[0]
    for k in range(4):
        first = (rep ^ k) * 2
        for o in range(12):
            block = (dot_nt(daggs[k][...], feats[o][...]) * (1.0 / 16.0)).astype(jnp.bfloat16)
            for a in range(2):
                for b in range(2):
                    grid_ref[(first + a) * 24 + 2 * o + b] = block[
                        a * 128 : (a + 1) * 128, b * 128 : (b + 1) * 128
                    ]

    def send(k, c):
        pltpu.make_async_copy(grid_ref.at[row_ref[k] * 24 + loc_ref[k]], out_ref.at[k], sem).start()
        return c

    def blank(k, c):
        pltpu.make_async_copy(zero_ref, out_ref.at[k], sem).start()
        return c

    lax.fori_loop(0, count_ref[0], send, 0)
    lax.fori_loop(count_ref[0], slots, blank, 0)

    def wait(k, c):
        pltpu.make_async_copy(zero_ref, out_ref.at[k], sem).wait()
        return c

    lax.fori_loop(0, slots, wait, 0)


def finish_kernel(base_ref, own_ref, *refs):
    terms, out_ref = refs[:-1], refs[-1]
    total = own_ref[...]
    for t in terms:
        total = total + t[...].astype(jnp.float32)
    out_ref[...] = (base_ref[...] + total.T).astype(jnp.bfloat16)


def shape(s, t=jnp.bfloat16):
    return jax.ShapeDtypeStruct(s, t)


def call(kernel, name, outs, ins, flops=0, moved=1 << 20, scratch=(), limit=24):
    return pl.pallas_call(
        kernel,
        out_shape=outs,
        in_specs=ins,
        out_specs=jax.tree.map(lambda _: VMEM, outs),
        scratch_shapes=scratch,
        compiler_params=pltpu.CompilerParams(vmem_limit_bytes=limit << 20),
        cost_estimate=pl.CostEstimate(flops=flops, bytes_accessed=moved, transcendentals=0),
        name=name,
    )


def local(node_feats, tile_vals, tile_row, tile_col, tile_count, w_agg, w_self, bias, cotangent):
    n_blk, n_rep = lax.axis_size("blk"), lax.axis_size("rep")
    group = lax.axis_index("blk")
    half = (group // 4) & 1
    rep = lax.axis_index("rep").reshape(1).astype(jnp.int32)
    row = tile_row[0, 0]
    count = tile_count[0]
    away = (lax.div(tile_col[0, 0], 2) - group + n_blk) & (n_blk - 1)
    place = jnp.zeros_like(away)
    for d in DISTANCES[1:]:
        place = place + (away >= d).astype(jnp.int32)
    place = jnp.where((half == 1) & (away == 4), 9, jnp.where((half == 1) & (away == 60), 3, place))
    loc = (2 * place + lax.rem(tile_col[0, 0], 2)).astype(jnp.int32)

    def move(x, source):
        pairs = [(source(g) * n_rep + r, g * n_rep + r) for g in range(n_blk) for r in range(n_rep)]
        return lax.ppermute(x, ("blk", "rep"), pairs)

    def from_blk(x, d):
        return move(x, lambda g: (g + d) % n_blk)

    def flip(x):
        return move(x, lambda g: g ^ 4)

    def from_plane(x, sign):
        return move(x, lambda g: (g + (8 * sign if g & 4 else -8 * sign)) % n_blk)

    def to_rep(x, k):
        return lax.ppermute(x, "rep", [(i, i ^ k) for i in range(n_rep)])

    def add(a, b):
        return (a.astype(jnp.float32) + b.astype(jnp.float32)).astype(jnp.bfloat16)

    up, down = from_blk(node_feats, 8), from_blk(node_feats, -8)
    right, left = from_blk(node_feats, 1), from_blk(node_feats, -1)
    across = flip(node_feats)
    up2, down2 = from_blk(up, 8), from_blk(down, -8)
    right2, left2 = from_blk(right, 1), from_blk(left, -1)
    across2 = from_plane(across, 1)
    up4 = from_blk(up2, 16)
    feats = [node_feats, right, right2, across, up, up2, up4, down2, down, across2, left2, left]

    dense = call(
        build_kernel, "build", shape((1024, 3072)), [SMEM, SMEM, SMEM, HBM], moved=10 << 20,
        scratch=[
            pltpu.VMEM((192, 128, 128), jnp.float32),
            pltpu.VMEM((128, 128, 128), jnp.bfloat16),
            pltpu.SemaphoreType.DMA((4,)),
        ],
        limit=36,
    )(row, loc, count, pltpu.with_memory_space_constraint(tile_vals[0, 0], pltpu.HBM))

    block = (256, 256)
    work = 2 * 1024 * 3072 * 256

    def forward(ks, types):
        return call(
            functools.partial(forward_kernel, ks), "forward", [shape(block, t) for t in types],
            [SMEM, VMEM] + [VMEM] * 12, flops=work // 2, moved=4 << 20,
        )(rep, dense, *feats)

    near, far = forward((1, 3), (jnp.bfloat16, jnp.bfloat16))
    near, far = to_rep(near, 1), to_rep(far, 1)
    own, other = forward((0, 2), (jnp.float32, jnp.float32))
    far = to_rep(add(other, far), 2)

    quarter = shape((256, 128), jnp.float32)
    updated, dagg, base, g0, g1, g2, g3 = call(
        update_kernel, "update",
        [shape(block), shape(block), shape(block, jnp.float32)] + [quarter] * 4,
        [SMEM] + [VMEM] * 8, flops=12 * 256**3, moved=2 << 20,
        scratch=[pltpu.VMEM((4, 256, 128), jnp.float32)],
    )(rep, own, near, far, node_feats, cotangent, w_agg, w_self, bias.reshape(1, 256))

    def gather_rep(x):
        x2, x1 = to_rep(x, 2), to_rep(x, 1)
        return [x, x1, x2, to_rep(x2, 1)]

    daggs = gather_rep(dagg)
    terms = call(
        scatter_kernel, "scatter", [shape(block, jnp.float32)] + [shape(block)] * 11,
        [SMEM] + [VMEM] * 5, flops=work, moved=8 << 20,
    )(rep, dense, *daggs)

    up2_sum = add(terms[5], from_blk(terms[6], -16))
    up_sum = add(terms[4], from_blk(up2_sum, -8))
    down_sum = add(terms[8], from_blk(terms[7], 8))
    right_sum = add(terms[1], from_blk(terms[2], -1))
    left_sum = add(terms[11], from_blk(terms[10], 1))
    across_sum = add(terms[3], from_plane(terms[9], -1))
    arrived = [
        from_blk(up_sum, -8), from_blk(down_sum, 8), from_blk(right_sum, -1), from_blk(left_sum, 1), flip(across_sum)
    ]

    tile_grads = pl.pallas_call(
        tile_grads_kernel,
        out_shape=shape((128, 128, 128)),
        in_specs=[SMEM] * 4 + [VMEM] * 16,
        out_specs=ANY,
        scratch_shapes=[
            pltpu.VMEM((192, 128, 128), jnp.bfloat16),
            pltpu.VMEM((128, 128), jnp.bfloat16),
            pltpu.SemaphoreType.DMA,
        ],
        compiler_params=pltpu.CompilerParams(vmem_limit_bytes=24 << 20),
        cost_estimate=pl.CostEstimate(flops=work, bytes_accessed=8 << 20, transcendentals=0),
        name="tile_grads",
    )(rep, row, loc, count, *daggs, *feats)

    feat_grad = call(finish_kernel, "finish", shape(block), [VMEM] * 7)(base, terms[0], *arrived)

    mine = g0 + to_rep(g1, 1)
    theirs = g2 + to_rep(g3, 1)
    mine = mine + to_rep(theirs, 2)
    pieces = lax.all_to_all(mine.reshape(n_blk, 4, 128), "blk", 0, 0, tiled=True)
    spread = call(spread_kernel, "spread", shape((n_blk, 4, 128), jnp.float32), [VMEM])(pieces)
    whole = lax.all_to_all(spread, "blk", 0, 0, tiled=True).reshape(256, 128)
    weight_grads = call(
        join_kernel, "join", shape((2, 256, 256), jnp.float32), [SMEM] + [VMEM] * 4,
        scratch=[pltpu.VMEM((4, 256, 128), jnp.float32)],
    )(rep, *gather_rep(whole))
    return updated, feat_grad, tile_grads.reshape(1, 1, 128, 128, 128), weight_grads


def solution(mesh):
    in_specs = (
        P(("blk", "rep"), None),
        P("blk", "rep", None, None, None),
        P("blk", "rep", None),
        P("blk", "rep", None),
        P("blk", "rep"),
        P(),
        P(),
        P(),
        P(("blk", "rep"), None),
    )
    out_specs = (
        P(("blk", "rep"), None),
        P(("blk", "rep"), None),
        P("blk", "rep", None, None, None),
        P(),
    )
    return jax.shard_map(local, mesh=mesh, in_specs=in_specs, out_specs=out_specs, check_vma=False)
```

```python
import functools

import jax
import jax.numpy as jnp
from jax import lax
from jax.experimental import pallas as pl
from jax.experimental.pallas import tpu as pltpu
from jax.sharding import PartitionSpec as P

DISTANCES = (0, 1, 2, 4, 8, 16, 32, 48, 56, 60, 62, 63)
VMEM = pl.BlockSpec(memory_space=pltpu.VMEM)
SMEM = pl.BlockSpec(memory_space=pltpu.SMEM)
ANY = pl.BlockSpec(memory_space=pl.ANY)
HBM = pl.BlockSpec(memory_space=pltpu.HBM)


def dot_nt(a, b):
    return lax.dot_general(a, b, (((1,), (1,)), ((), ())), preferred_element_type=jnp.float32)


def dot_tn(a, b):
    return lax.dot_general(a, b, (((0,), (0,)), ((), ())), preferred_element_type=jnp.float32)


def build_kernel(row_ref, loc_ref, count_ref, vals_ref, dense_ref, acc_ref, held_ref, sems):
    parts = sems.shape[0]
    share = held_ref.shape[0] // parts
    copies = [
        pltpu.make_async_copy(
            vals_ref.at[pl.ds(p * share, share)], held_ref.at[pl.ds(p * share, share)], sems.at[p]
        )
        for p in range(parts)
    ]
    for copy in copies:
        copy.start()
    col_tiles = dense_ref.shape[1] // 128
    row_tiles = dense_ref.shape[0] // 128

    def clear(i, c):
        acc_ref[i] = jnp.zeros((128, 128), jnp.float32)
        return c

    lax.fori_loop(0, row_tiles * col_tiles, clear, 0)

    def add(k, c):
        at = row_ref[k] * col_tiles + loc_ref[k]
        acc_ref[at] = acc_ref[at] + held_ref[k].astype(jnp.float32)
        return c

    for p, copy in enumerate(copies):
        copy.wait()
        lax.fori_loop(p * share, jnp.minimum((p + 1) * share, count_ref[0]), add, 0)

    def cast(q, c):
        rows = pl.ds(pl.multiple_of(q * 128, 128), 128)
        for t in range(col_tiles):
            dense_ref[rows, t * 128 : (t + 1) * 128] = acc_ref[q * col_tiles + t].astype(jnp.bfloat16)
        return c

    lax.fori_loop(0, row_tiles, cast, 0)


def group_rows(rep, k):
    return pl.ds(pl.multiple_of((rep ^ k) * 256, 256), 256)


def forward_kernel(ks, rep_ref, dense_ref, *refs):
    feats, outs = refs[:12], refs[12:]
    for k, out in zip(ks, outs):
        total = jnp.zeros((256, 256), jnp.float32)
        for o in range(12):
            total = total + jnp.dot(
                dense_ref[group_rows(rep_ref[0], k), o * 256 : (o + 1) * 256],
                feats[o][...],
                preferred_element_type=jnp.float32,
            )
        out[...] = total.astype(out.dtype)


def update_kernel(
    rep_ref, own_ref, sib_ref, far_ref, x_ref, cot_ref, wa_ref, ws_ref, b_ref,
    upd_ref, dagg_ref, base_ref, g0_ref, g1_ref, g2_ref, g3_ref, grads_ref,
):
    agg = own_ref[...] + sib_ref[...].astype(jnp.float32) + far_ref[...].astype(jnp.float32)
    agg_b = agg.astype(jnp.bfloat16)
    x = x_ref[...]
    pre = (
        jnp.dot(agg_b, wa_ref[...], preferred_element_type=jnp.float32)
        + jnp.dot(x, ws_ref[...], preferred_element_type=jnp.float32)
        + b_ref[...]
    )
    s = 1.0 / (1.0 + jnp.exp(-pre))
    upd_ref[...] = (x.astype(jnp.float32) + pre * s).astype(jnp.bfloat16)
    cot = cot_ref[...].astype(jnp.float32)
    dpre = (cot * (s * (1.0 + pre * (1.0 - s)))).astype(jnp.bfloat16)
    dagg_ref[...] = dot_nt(dpre, wa_ref[...]).astype(jnp.bfloat16)
    base_ref[...] = cot + dot_nt(dpre, ws_ref[...])
    scale = 1.0 / 256.0
    for i, a in enumerate((agg_b, x)):
        total = dot_tn(a, dpre) * scale
        grads_ref[2 * i] = total[:, :128]
        grads_ref[2 * i + 1] = total[:, 128:]
    for k, out in enumerate((g0_ref, g1_ref, g2_ref, g3_ref)):
        out[...] = grads_ref[rep_ref[0] ^ k]


def scatter_kernel(rep_ref, group_ref, dense_ref, d0, d1, d2, d3, *outs):
    turned = [d[...].T for d in (d0, d1, d2, d3)]
    group = group_ref[0]
    line, half = group & 3, (group // 4) & 1
    swaps = (line >= 2, (line >= 2) ^ (half == 1))
    for o in range(12):
        columns = pl.ds(o * 256, 256)
        if o in (2, 3, 9, 10):
            place = jnp.where(swaps[o & 1], 12 - o, o)
            columns = pl.ds(pl.multiple_of(place * 256, 256), 256)
        total = jnp.zeros((256, 256), jnp.float32)
        for k in range(4):
            total = total + jnp.dot(
                turned[k],
                dense_ref[group_rows(rep_ref[0], k), columns],
                preferred_element_type=jnp.float32,
            )
        outs[o][...] = total.astype(outs[o].dtype)


def spread_kernel(pieces_ref, out_ref):
    total = jnp.sum(pieces_ref[...], axis=0)
    out_ref[...] = jnp.broadcast_to(total[None], out_ref.shape)


def join_kernel(rep_ref, q0, q1, q2, q3, out_ref, quarters_ref):
    for k, q in enumerate((q0, q1, q2, q3)):
        quarters_ref[rep_ref[0] ^ k] = q[...]
    for i in range(2):
        out_ref[i, :, :128] = quarters_ref[2 * i]
        out_ref[i, :, 128:] = quarters_ref[2 * i + 1]


def tile_grads_kernel(rep_ref, row_ref, loc_ref, count_ref, d0, d1, d2, d3, *refs):
    feats, out_ref, (grid_ref, all_ref, zero_ref, sem) = refs[:12], refs[12], refs[13:]
    daggs = (d0, d1, d2, d3)
    rep = rep_ref[0]
    zero_ref[...] = jnp.zeros_like(zero_ref)
    slots = out_ref.shape[0]
    for k in range(4):
        all_ref[group_rows(rep, k)] = daggs[k][...]
    for o in range(12):
        block = (dot_nt(all_ref[...], feats[o][...]) * (1.0 / 16.0)).astype(jnp.bfloat16)
        for q in range(8):
            for b in range(2):
                grid_ref[q * 24 + 2 * o + b] = block[q * 128 : (q + 1) * 128, b * 128 : (b + 1) * 128]

    def send(k, c):
        pltpu.make_async_copy(grid_ref.at[row_ref[k] * 24 + loc_ref[k]], out_ref.at[k], sem).start()
        return c

    def blank(k, c):
        pltpu.make_async_copy(zero_ref, out_ref.at[k], sem).start()
        return c

    lax.fori_loop(0, count_ref[0], send, 0)
    lax.fori_loop(count_ref[0], slots, blank, 0)

    pltpu.make_async_copy(out_ref, out_ref, sem).wait()


def finish_kernel(base_ref, own_ref, *refs):
    terms, out_ref = refs[:-1], refs[-1]
    total = own_ref[...]
    for t in terms:
        total = total + t[...].astype(jnp.float32)
    out_ref[...] = (base_ref[...] + total.T).astype(jnp.bfloat16)


def shape(s, t=jnp.bfloat16):
    return jax.ShapeDtypeStruct(s, t)


def call(kernel, name, outs, ins, flops=0, moved=1 << 20, scratch=(), limit=24):
    return pl.pallas_call(
        kernel,
        out_shape=outs,
        in_specs=ins,
        out_specs=jax.tree.map(lambda _: VMEM, outs),
        scratch_shapes=scratch,
        compiler_params=pltpu.CompilerParams(vmem_limit_bytes=limit << 20),
        cost_estimate=pl.CostEstimate(flops=flops, bytes_accessed=moved, transcendentals=0),
        name=name,
    )


def local(node_feats, tile_vals, tile_row, tile_col, tile_count, w_agg, w_self, bias, cotangent):
    n_blk, n_rep = lax.axis_size("blk"), lax.axis_size("rep")
    group = lax.axis_index("blk")
    half, line = (group // 4) & 1, group & 3
    rep = lax.axis_index("rep").reshape(1).astype(jnp.int32)
    ring = group.reshape(1).astype(jnp.int32)
    row = tile_row[0, 0]
    count = tile_count[0]
    away = (lax.div(tile_col[0, 0], 2) - group + n_blk) & (n_blk - 1)
    place = jnp.zeros_like(away)
    for d in DISTANCES[1:]:
        place = place + (away >= d).astype(jnp.int32)
    swapped = (line >= 2) & ((away == 4) | (away == 60) | (away == 2) | (away == 62))
    place = jnp.where(swapped, 12 - place, place)
    loc = (2 * place + lax.rem(tile_col[0, 0], 2)).astype(jnp.int32)

    def move(x, source):
        pairs = [(source(g) * n_rep + r, g * n_rep + r) for g in range(n_blk) for r in range(n_rep)]
        return lax.ppermute(x, ("blk", "rep"), pairs)

    def from_blk(x, d):
        return move(x, lambda g: (g + d) % n_blk)

    def flip(x):
        return move(x, lambda g: g ^ 4)

    def from_plane(x, sign):
        return move(x, lambda g: (g + (8 * sign if g & 4 else -8 * sign)) % n_blk)

    def to_rep(x, k):
        return lax.ppermute(x, "rep", [(i, i ^ k) for i in range(n_rep)])

    def add(a, b):
        return (a.astype(jnp.float32) + b.astype(jnp.float32)).astype(jnp.bfloat16)

    def cross(g):
        return (g + 4 if g & 3 < 2 else g - 4) % n_blk

    def other(g):
        return (g - 4 if g & 3 < 2 else g + 4) % n_blk

    crossing = move(node_feats, cross)
    up, down = from_blk(node_feats, 8), from_blk(node_feats, -8)
    over2 = move(node_feats, lambda g: g ^ 2)
    up2, down2 = from_blk(up, 8), from_blk(down, -8)
    right = move(jnp.where(line == 0, crossing, node_feats), lambda g: g & ~3 | (g + 1) & 3)
    left = move(jnp.where(line == 3, crossing, node_feats), lambda g: g & ~3 | (g - 1) & 3)
    cross2 = move(crossing, lambda g: g ^ 2)
    rest = move(node_feats, other)
    up4 = from_blk(up2, 16)
    feats = [node_feats, right, over2, crossing, up, up2, up4, down2, down, rest, cross2, left]

    dense = call(
        build_kernel, "build", shape((1024, 3072)), [SMEM, SMEM, SMEM, HBM], moved=10 << 20,
        scratch=[
            pltpu.VMEM((192, 128, 128), jnp.float32),
            pltpu.VMEM((128, 128, 128), jnp.bfloat16),
            pltpu.SemaphoreType.DMA((4,)),
        ],
        limit=36,
    )(row, loc, count, pltpu.with_memory_space_constraint(tile_vals[0, 0], pltpu.HBM))

    block = (256, 256)
    work = 2 * 1024 * 3072 * 256

    def forward(ks, types):
        return call(
            functools.partial(forward_kernel, ks), "forward", [shape(block, t) for t in types],
            [SMEM, VMEM] + [VMEM] * 12, flops=work // 2, moved=4 << 20,
        )(rep, dense, *feats)

    near, far = forward((1, 3), (jnp.bfloat16, jnp.bfloat16))
    near, far = to_rep(near, 1), to_rep(far, 1)
    own, other = forward((0, 2), (jnp.float32, jnp.float32))
    far = to_rep(add(other, far), 2)

    quarter = shape((256, 128), jnp.float32)
    updated, dagg, base, g0, g1, g2, g3 = call(
        update_kernel, "update",
        [shape(block), shape(block), shape(block, jnp.float32)] + [quarter] * 4,
        [SMEM] + [VMEM] * 8, flops=12 * 256**3, moved=2 << 20,
        scratch=[pltpu.VMEM((4, 256, 128), jnp.float32)],
    )(rep, own, near, far, node_feats, cotangent, w_agg, w_self, bias.reshape(1, 256))

    def gather_rep(x):
        x2, x1 = to_rep(x, 2), to_rep(x, 1)
        return [x, x1, x2, to_rep(x2, 1)]

    daggs = gather_rep(dagg)
    terms = call(
        scatter_kernel, "scatter", [shape(block, jnp.float32)] + [shape(block)] * 11,
        [SMEM] * 2 + [VMEM] * 5, flops=work, moved=8 << 20,
    )(rep, ring, dense, *daggs)

    up2_sum = add(terms[5], from_blk(terms[6], -16))
    up_sum = add(terms[4], from_blk(up2_sum, -8))
    down_sum = add(terms[8], from_blk(terms[7], 8))
    right_sum = add(terms[1], from_blk(terms[2], -1))
    left_sum = add(terms[11], from_blk(terms[10], 1))
    across_sum = add(terms[3], from_plane(terms[9], -1))
    arrived = [
        from_blk(up_sum, -8), from_blk(down_sum, 8), from_blk(right_sum, -1), from_blk(left_sum, 1), flip(across_sum)
    ]

    tile_grads = pl.pallas_call(
        tile_grads_kernel,
        out_shape=shape((128, 128, 128)),
        in_specs=[SMEM] * 4 + [VMEM] * 16,
        out_specs=ANY,
        scratch_shapes=[
            pltpu.VMEM((192, 128, 128), jnp.bfloat16),
            pltpu.VMEM((1024, 256), jnp.bfloat16),
            pltpu.VMEM((128, 128), jnp.bfloat16),
            pltpu.SemaphoreType.DMA,
        ],
        compiler_params=pltpu.CompilerParams(vmem_limit_bytes=24 << 20),
        cost_estimate=pl.CostEstimate(flops=work, bytes_accessed=8 << 20, transcendentals=0),
        name="tile_grads",
    )(rep, row, loc, count, *daggs, *feats)

    feat_grad = call(finish_kernel, "finish", shape(block), [VMEM] * 7)(base, terms[0], *arrived)

    mine = g0 + to_rep(g1, 1)
    theirs = g2 + to_rep(g3, 1)
    mine = mine + to_rep(theirs, 2)
    pieces = lax.all_to_all(mine.reshape(n_blk, 4, 128), "blk", 0, 0, tiled=True)
    spread = call(spread_kernel, "spread", shape((n_blk, 4, 128), jnp.float32), [VMEM])(pieces)
    whole = lax.all_to_all(spread, "blk", 0, 0, tiled=True).reshape(256, 128)
    weight_grads = call(
        join_kernel, "join", shape((2, 256, 256), jnp.float32), [SMEM] + [VMEM] * 4,
        scratch=[pltpu.VMEM((4, 256, 128), jnp.float32)],
    )(rep, *gather_rep(whole))
    return updated, feat_grad, tile_grads.reshape(1, 1, 128, 128, 128), weight_grads


def solution(mesh):
    in_specs = (
        P(("blk", "rep"), None),
        P("blk", "rep", None, None, None),
        P("blk", "rep", None),
        P("blk", "rep", None),
        P("blk", "rep"),
        P(),
        P(),
        P(),
        P(("blk", "rep"), None),
    )
    out_specs = (
        P(("blk", "rep"), None),
        P(("blk", "rep"), None),
        P("blk", "rep", None, None, None),
        P(),
    )
    return jax.shard_map(local, mesh=mesh, in_specs=in_specs, out_specs=out_specs, check_vma=False)
```

```python
import functools

import jax
import jax.numpy as jnp
from jax import lax
from jax.experimental import pallas as pl
from jax.experimental.pallas import tpu as pltpu
from jax.sharding import PartitionSpec as P

DISTANCES = (0, 1, 2, 4, 8, 16, 32, 48, 56, 60, 62, 63)
VMEM = pl.BlockSpec(memory_space=pltpu.VMEM)
SMEM = pl.BlockSpec(memory_space=pltpu.SMEM)
ANY = pl.BlockSpec(memory_space=pl.ANY)
HBM = pl.BlockSpec(memory_space=pltpu.HBM)


def dot_nt(a, b):
    return lax.dot_general(a, b, (((1,), (1,)), ((), ())), preferred_element_type=jnp.float32)


def dot_tn(a, b):
    return lax.dot_general(a, b, (((0,), (0,)), ((), ())), preferred_element_type=jnp.float32)


def build_kernel(at_ref, count_ref, vals_ref, dense_ref, acc_ref, held_ref, sems):
    parts = sems.shape[0]
    share = held_ref.shape[0] // parts
    copies = [
        pltpu.make_async_copy(
            vals_ref.at[pl.ds(p * share, share)], held_ref.at[pl.ds(p * share, share)], sems.at[p]
        )
        for p in range(parts)
    ]
    for copy in copies:
        copy.start()
    col_tiles = dense_ref.shape[1] // 128
    row_tiles = dense_ref.shape[0] // 128

    def clear(i, c):
        acc_ref[i] = jnp.zeros((128, 128), jnp.float32)
        return c

    lax.fori_loop(0, row_tiles * col_tiles, clear, 0)

    def add(k, c):
        at = at_ref[k]
        acc_ref[at] = acc_ref[at] + held_ref[k].astype(jnp.float32)
        return c

    for p, copy in enumerate(copies):
        copy.wait()
        lax.fori_loop(p * share, jnp.minimum((p + 1) * share, count_ref[0]), add, 0)

    def cast(q, c):
        rows = pl.ds(pl.multiple_of(q * 128, 128), 128)
        for t in range(col_tiles):
            dense_ref[rows, t * 128 : (t + 1) * 128] = acc_ref[q * col_tiles + t].astype(jnp.bfloat16)
        return c

    lax.fori_loop(0, row_tiles, cast, 0)


def group_rows(rep, k):
    return pl.ds(pl.multiple_of((rep ^ k) * 256, 256), 256)


def forward_kernel(ks, rep_ref, dense_ref, *refs):
    feats, outs = refs[:12], refs[12:]
    for k, out in zip(ks, outs):
        total = jnp.zeros((256, 256), jnp.float32)
        for o in range(12):
            total = total + jnp.dot(
                dense_ref[group_rows(rep_ref[0], k), o * 256 : (o + 1) * 256],
                feats[o][...],
                preferred_element_type=jnp.float32,
            )
        out[...] = total.astype(out.dtype)


def update_kernel(
    rep_ref, own_ref, sib_ref, far_ref, x_ref, cot_ref, wa_ref, ws_ref, b_ref,
    upd_ref, dagg_ref, base_ref, g0_ref, g1_ref, g2_ref, g3_ref, grads_ref,
):
    agg = own_ref[...] + sib_ref[...].astype(jnp.float32) + far_ref[...].astype(jnp.float32)
    agg_b = agg.astype(jnp.bfloat16)
    x = x_ref[...]
    pre = (
        jnp.dot(agg_b, wa_ref[...], preferred_element_type=jnp.float32)
        + jnp.dot(x, ws_ref[...], preferred_element_type=jnp.float32)
        + b_ref[...]
    )
    s = 1.0 / (1.0 + jnp.exp(-pre))
    upd_ref[...] = (x.astype(jnp.float32) + pre * s).astype(jnp.bfloat16)
    cot = cot_ref[...].astype(jnp.float32)
    dpre = (cot * (s * (1.0 + pre * (1.0 - s)))).astype(jnp.bfloat16)
    dagg_ref[...] = dot_nt(dpre, wa_ref[...]).astype(jnp.bfloat16)
    base_ref[...] = cot + dot_nt(dpre, ws_ref[...])
    scale = 1.0 / 256.0
    for i, a in enumerate((agg_b, x)):
        total = dot_tn(a, dpre) * scale
        grads_ref[2 * i] = total[:, :128]
        grads_ref[2 * i + 1] = total[:, 128:]
    for k, out in enumerate((g0_ref, g1_ref, g2_ref, g3_ref)):
        out[...] = grads_ref[rep_ref[0] ^ k]


def scatter_kernel(rep_ref, group_ref, dense_ref, d0, d1, d2, d3, *outs):
    turned = [d[...].T for d in (d0, d1, d2, d3)]
    group = group_ref[0]
    line, half = group & 3, (group // 4) & 1
    swaps = (line >= 2, (line >= 2) ^ (half == 1))
    for o in range(12):
        columns = pl.ds(o * 256, 256)
        if o in (2, 3, 9, 10):
            place = jnp.where(swaps[o & 1], 12 - o, o)
            columns = pl.ds(pl.multiple_of(place * 256, 256), 256)
        total = jnp.zeros((256, 256), jnp.float32)
        for k in range(4):
            total = total + jnp.dot(
                turned[k],
                dense_ref[group_rows(rep_ref[0], k), columns],
                preferred_element_type=jnp.float32,
            )
        outs[o][...] = total.astype(outs[o].dtype)


def spread_kernel(pieces_ref, out_ref):
    total = jnp.sum(pieces_ref[...], axis=0)
    out_ref[...] = jnp.broadcast_to(total[None], out_ref.shape)


def tile_grads_kernel(rep_ref, at_ref, count_ref, d0, d1, d2, d3, *refs):
    feats, out_ref, (grid_ref, all_ref, zero_ref, sem) = refs[:12], refs[12], refs[13:]
    daggs = (d0, d1, d2, d3)
    rep = rep_ref[0]
    zero_ref[...] = jnp.zeros_like(zero_ref)
    slots = out_ref.shape[0]
    for k in range(4):
        all_ref[group_rows(rep, k)] = daggs[k][...]
    for o in range(12):
        block = (dot_nt(all_ref[...], feats[o][...]) * (1.0 / 16.0)).astype(jnp.bfloat16)
        for q in range(8):
            for b in range(2):
                grid_ref[q * 24 + 2 * o + b] = block[q * 128 : (q + 1) * 128, b * 128 : (b + 1) * 128]

    def send(k, c):
        pltpu.make_async_copy(grid_ref.at[at_ref[k]], out_ref.at[k], sem).start()
        return c

    def blank(k, c):
        pltpu.make_async_copy(zero_ref, out_ref.at[k], sem).start()
        return c

    lax.fori_loop(0, count_ref[0], send, 0)
    lax.fori_loop(count_ref[0], slots, blank, 0)

    pltpu.make_async_copy(out_ref, out_ref, sem).wait()


def finish_kernel(rep_ref, base_ref, own_ref, *refs):
    terms, quarters, (out_ref, grads_ref, held_ref) = refs[:5], refs[5:9], refs[9:]
    total = own_ref[...]
    for t in terms:
        total = total + t[...].astype(jnp.float32)
    out_ref[...] = (base_ref[...] + total.T).astype(jnp.bfloat16)
    for k, q in enumerate(quarters):
        held_ref[rep_ref[0] ^ k] = q[...]
    for i in range(2):
        grads_ref[i, :, :128] = held_ref[2 * i]
        grads_ref[i, :, 128:] = held_ref[2 * i + 1]


def shape(s, t=jnp.bfloat16):
    return jax.ShapeDtypeStruct(s, t)


def call(kernel, name, outs, ins, flops=0, moved=1 << 20, scratch=(), limit=24):
    return pl.pallas_call(
        kernel,
        out_shape=outs,
        in_specs=ins,
        out_specs=jax.tree.map(lambda _: VMEM, outs),
        scratch_shapes=scratch,
        compiler_params=pltpu.CompilerParams(vmem_limit_bytes=limit << 20),
        cost_estimate=pl.CostEstimate(flops=flops, bytes_accessed=moved, transcendentals=0),
        name=name,
    )


def local(node_feats, tile_vals, tile_row, tile_col, tile_count, w_agg, w_self, bias, cotangent):
    n_blk, n_rep = lax.axis_size("blk"), lax.axis_size("rep")
    group = lax.axis_index("blk")
    half, line = (group // 4) & 1, group & 3
    rep = lax.axis_index("rep").reshape(1).astype(jnp.int32)
    ring = group.reshape(1).astype(jnp.int32)
    count = tile_count[0]
    away = (lax.div(tile_col[0, 0], 2) - group + n_blk) & (n_blk - 1)
    place = jnp.zeros_like(away)
    for d in DISTANCES[1:]:
        place = place + (away >= d).astype(jnp.int32)
    swapped = (line >= 2) & ((away == 4) | (away == 60) | (away == 2) | (away == 62))
    place = jnp.where(swapped, 12 - place, place)
    at = (24 * tile_row[0, 0] + 2 * place + lax.rem(tile_col[0, 0], 2)).astype(jnp.int32)

    def move(x, source):
        pairs = [(source(g) * n_rep + r, g * n_rep + r) for g in range(n_blk) for r in range(n_rep)]
        return lax.ppermute(x, ("blk", "rep"), pairs)

    def from_blk(x, d):
        return move(x, lambda g: (g + d) % n_blk)

    def flip(x):
        return move(x, lambda g: g ^ 4)

    def from_plane(x, sign):
        return move(x, lambda g: (g + (8 * sign if g & 4 else -8 * sign)) % n_blk)

    def to_rep(x, k):
        return lax.ppermute(x, "rep", [(i, i ^ k) for i in range(n_rep)])

    def add(a, b):
        return (a.astype(jnp.float32) + b.astype(jnp.float32)).astype(jnp.bfloat16)

    def cross(g):
        return (g + 4 if g & 3 < 2 else g - 4) % n_blk

    def other(g):
        return (g - 4 if g & 3 < 2 else g + 4) % n_blk

    crossing = move(node_feats, cross)
    up, down = from_blk(node_feats, 8), from_blk(node_feats, -8)
    over2 = move(node_feats, lambda g: g ^ 2)
    up2, down2 = from_blk(up, 8), from_blk(down, -8)
    right = move(jnp.where(line == 0, crossing, node_feats), lambda g: g & ~3 | (g + 1) & 3)
    left = move(jnp.where(line == 3, crossing, node_feats), lambda g: g & ~3 | (g - 1) & 3)
    cross2 = move(crossing, lambda g: g ^ 2)
    rest = move(node_feats, other)
    up4 = from_blk(up2, 16)
    feats = [node_feats, right, over2, crossing, up, up2, up4, down2, down, rest, cross2, left]

    dense = call(
        build_kernel, "build", shape((1024, 3072)), [SMEM, SMEM, HBM], moved=10 << 20,
        scratch=[
            pltpu.VMEM((192, 128, 128), jnp.float32),
            pltpu.VMEM((128, 128, 128), jnp.bfloat16),
            pltpu.SemaphoreType.DMA((4,)),
        ],
        limit=36,
    )(at, count, pltpu.with_memory_space_constraint(tile_vals[0, 0], pltpu.HBM))

    block = (256, 256)
    work = 2 * 1024 * 3072 * 256

    def forward(ks, types):
        return call(
            functools.partial(forward_kernel, ks), "forward", [shape(block, t) for t in types],
            [SMEM, VMEM] + [VMEM] * 12, flops=work // 2, moved=4 << 20,
        )(rep, dense, *feats)

    near, far = forward((1, 3), (jnp.bfloat16, jnp.bfloat16))
    near, far = to_rep(near, 1), to_rep(far, 1)
    own, other = forward((0, 2), (jnp.float32, jnp.float32))
    far = to_rep(add(other, far), 2)

    quarter = shape((256, 128), jnp.float32)
    updated, dagg, base, g0, g1, g2, g3 = call(
        update_kernel, "update",
        [shape(block), shape(block), shape(block, jnp.float32)] + [quarter] * 4,
        [SMEM] + [VMEM] * 8, flops=12 * 256**3, moved=2 << 20,
        scratch=[pltpu.VMEM((4, 256, 128), jnp.float32)],
    )(rep, own, near, far, node_feats, cotangent, w_agg, w_self, bias.reshape(1, 256))

    def gather_rep(x):
        x2, x1 = to_rep(x, 2), to_rep(x, 1)
        return [x, x1, x2, to_rep(x2, 1)]

    daggs = gather_rep(dagg)
    terms = call(
        scatter_kernel, "scatter", [shape(block, jnp.float32)] + [shape(block)] * 11,
        [SMEM] * 2 + [VMEM] * 5, flops=work, moved=8 << 20,
    )(rep, ring, dense, *daggs)

    up2_sum = add(terms[5], from_blk(terms[6], -16))
    up_sum = add(terms[4], from_blk(up2_sum, -8))
    down_sum = add(terms[8], from_blk(terms[7], 8))
    right_sum = add(terms[1], from_blk(terms[2], -1))
    left_sum = add(terms[11], from_blk(terms[10], 1))
    across_sum = add(terms[3], from_plane(terms[9], -1))
    arrived = [
        from_blk(up_sum, -8), from_blk(down_sum, 8), from_blk(right_sum, -1), from_blk(left_sum, 1), flip(across_sum)
    ]

    tile_grads = pl.pallas_call(
        tile_grads_kernel,
        out_shape=shape((128, 128, 128)),
        in_specs=[SMEM] * 3 + [VMEM] * 16,
        out_specs=ANY,
        scratch_shapes=[
            pltpu.VMEM((192, 128, 128), jnp.bfloat16),
            pltpu.VMEM((1024, 256), jnp.bfloat16),
            pltpu.VMEM((128, 128), jnp.bfloat16),
            pltpu.SemaphoreType.DMA,
        ],
        compiler_params=pltpu.CompilerParams(vmem_limit_bytes=24 << 20),
        cost_estimate=pl.CostEstimate(flops=work, bytes_accessed=8 << 20, transcendentals=0),
        name="tile_grads",
    )(rep, at, count, *daggs, *feats)

    mine = g0 + to_rep(g1, 1)
    theirs = g2 + to_rep(g3, 1)
    mine = mine + to_rep(theirs, 2)
    pieces = lax.all_to_all(mine.reshape(n_blk, 4, 128), "blk", 0, 0, tiled=True)
    spread = call(spread_kernel, "spread", shape((n_blk, 4, 128), jnp.float32), [VMEM])(pieces)
    whole = lax.all_to_all(spread, "blk", 0, 0, tiled=True).reshape(256, 128)
    feat_grad, weight_grads = call(
        finish_kernel, "finish", [shape(block), shape((2, 256, 256), jnp.float32)], [SMEM] + [VMEM] * 11,
        scratch=[pltpu.VMEM((4, 256, 128), jnp.float32)],
    )(rep, base, terms[0], *arrived, *gather_rep(whole))
    return updated, feat_grad, tile_grads.reshape(1, 1, 128, 128, 128), weight_grads


def solution(mesh):
    in_specs = (
        P(("blk", "rep"), None),
        P("blk", "rep", None, None, None),
        P("blk", "rep", None),
        P("blk", "rep", None),
        P("blk", "rep"),
        P(),
        P(),
        P(),
        P(("blk", "rep"), None),
    )
    out_specs = (
        P(("blk", "rep"), None),
        P(("blk", "rep"), None),
        P("blk", "rep", None, None, None),
        P(),
    )
    return jax.shard_map(local, mesh=mesh, in_specs=in_specs, out_specs=out_specs, check_vma=False)
```

```python
import functools

import jax
import jax.numpy as jnp
from jax import lax
from jax.experimental import pallas as pl
from jax.experimental.pallas import tpu as pltpu
from jax.sharding import PartitionSpec as P

DISTANCES = (0, 1, 2, 4, 8, 16, 32, 48, 56, 60, 62, 63)
VMEM = pl.BlockSpec(memory_space=pltpu.VMEM)
SMEM = pl.BlockSpec(memory_space=pltpu.SMEM)
ANY = pl.BlockSpec(memory_space=pl.ANY)
HBM = pl.BlockSpec(memory_space=pltpu.HBM)


def dot_nt(a, b):
    return lax.dot_general(a, b, (((1,), (1,)), ((), ())), preferred_element_type=jnp.float32)


def dot_tn(a, b):
    return lax.dot_general(a, b, (((0,), (0,)), ((), ())), preferred_element_type=jnp.float32)


def build_kernel(at_ref, count_ref, vals_ref, dense_ref, acc_ref, held_ref, sems):
    parts = sems.shape[0]
    share = held_ref.shape[0] // parts
    copies = [
        pltpu.make_async_copy(
            vals_ref.at[pl.ds(p * share, share)], held_ref.at[pl.ds(p * share, share)], sems.at[p]
        )
        for p in range(parts)
    ]
    for copy in copies:
        copy.start()
    col_tiles = dense_ref.shape[1] // 128
    row_tiles = dense_ref.shape[0] // 128

    def clear(i, c):
        acc_ref[i] = jnp.zeros((128, 128), jnp.float32)
        return c

    lax.fori_loop(0, row_tiles * col_tiles, clear, 0)

    def add(k, c):
        at = at_ref[k]
        acc_ref[at] = acc_ref[at] + held_ref[k].astype(jnp.float32)
        return c

    for p, copy in enumerate(copies):
        copy.wait()
        lax.fori_loop(p * share, jnp.minimum((p + 1) * share, count_ref[0]), add, 0)

    def cast(q, c):
        rows = pl.ds(pl.multiple_of(q * 128, 128), 128)
        for t in range(col_tiles):
            dense_ref[rows, t * 128 : (t + 1) * 128] = acc_ref[q * col_tiles + t].astype(jnp.bfloat16)
        return c

    lax.fori_loop(0, row_tiles, cast, 0)


def group_rows(rep, k):
    return pl.ds(pl.multiple_of((rep ^ k) * 256, 256), 256)


def forward_kernel(ks, rep_ref, dense_ref, *refs):
    feats, outs = refs[:12], refs[12:]
    for k, out in zip(ks, outs):
        total = jnp.zeros((256, 256), jnp.float32)
        for o in range(12):
            total = total + jnp.dot(
                dense_ref[group_rows(rep_ref[0], k), o * 256 : (o + 1) * 256],
                feats[o][...],
                preferred_element_type=jnp.float32,
            )
        out[...] = total.astype(out.dtype)


def update_kernel(
    rep_ref, own_ref, sib_ref, far_ref, x_ref, cot_ref, wa_ref, ws_ref, b_ref,
    upd_ref, dagg_ref, base_ref, g0_ref, g1_ref, g2_ref, g3_ref, grads_ref,
):
    agg = own_ref[...] + sib_ref[...].astype(jnp.float32) + far_ref[...].astype(jnp.float32)
    agg_b = agg.astype(jnp.bfloat16)
    x = x_ref[...]
    pre = (
        jnp.dot(agg_b, wa_ref[...], preferred_element_type=jnp.float32)
        + jnp.dot(x, ws_ref[...], preferred_element_type=jnp.float32)
        + b_ref[...]
    )
    s = 1.0 / (1.0 + jnp.exp(-pre))
    upd_ref[...] = (x.astype(jnp.float32) + pre * s).astype(jnp.bfloat16)
    cot = cot_ref[...].astype(jnp.float32)
    dpre = (cot * (s * (1.0 + pre * (1.0 - s)))).astype(jnp.bfloat16)
    dagg_ref[...] = dot_nt(dpre, wa_ref[...]).astype(jnp.bfloat16)
    base_ref[...] = cot + dot_nt(dpre, ws_ref[...])
    scale = 1.0 / 256.0
    for i, a in enumerate((agg_b, x)):
        total = dot_tn(a, dpre) * scale
        grads_ref[2 * i] = total[:, :128]
        grads_ref[2 * i + 1] = total[:, 128:]
    for k, out in enumerate((g0_ref, g1_ref, g2_ref, g3_ref)):
        out[...] = grads_ref[rep_ref[0] ^ k]


def scatter_kernel(rep_ref, group_ref, dense_ref, d0, d1, d2, d3, *outs):
    turned = [d[...].T for d in (d0, d1, d2, d3)]
    group = group_ref[0]
    line, half = group & 3, (group // 4) & 1
    swaps = (line >= 2, (line >= 2) ^ (half == 1))
    for o in range(12):
        columns = pl.ds(o * 256, 256)
        if o in (2, 3, 9, 10):
            place = jnp.where(swaps[o & 1], 12 - o, o)
            columns = pl.ds(pl.multiple_of(place * 256, 256), 256)
        total = jnp.zeros((256, 256), jnp.float32)
        for k in range(4):
            total = total + jnp.dot(
                turned[k],
                dense_ref[group_rows(rep_ref[0], k), columns],
                preferred_element_type=jnp.float32,
            )
        outs[o][...] = total.astype(outs[o].dtype)


def late_sum_kernel(a_ref, b_ref, after_ref, out_ref):
    out_ref[...] = (a_ref[...].astype(jnp.float32) + b_ref[...].astype(jnp.float32)).astype(jnp.bfloat16)


def fold_kernel(a_ref, b_ref, c_ref, after_ref, out_ref):
    out_ref[...] = a_ref[...] + b_ref[...] + c_ref[...]


def spread_kernel(pieces_ref, *refs):
    out_ref = refs[-1]
    total = jnp.sum(pieces_ref[...], axis=0)
    out_ref[...] = jnp.broadcast_to(total[None], out_ref.shape)


def tile_grads_kernel(rep_ref, at_ref, count_ref, d0, d1, d2, d3, *refs):
    feats, out_ref, (grid_ref, all_ref, zero_ref, sem) = refs[:12], refs[12], refs[13:]
    daggs = (d0, d1, d2, d3)
    rep = rep_ref[0]
    zero_ref[...] = jnp.zeros_like(zero_ref)
    slots = out_ref.shape[0]
    for k in range(4):
        all_ref[group_rows(rep, k)] = daggs[k][...]
    for o in range(12):
        block = (dot_nt(all_ref[...], feats[o][...]) * (1.0 / 16.0)).astype(jnp.bfloat16)
        for q in range(8):
            for b in range(2):
                grid_ref[q * 24 + 2 * o + b] = block[q * 128 : (q + 1) * 128, b * 128 : (b + 1) * 128]

    def send(k, c):
        pltpu.make_async_copy(grid_ref.at[at_ref[k]], out_ref.at[k], sem).start()
        return c

    def blank(k, c):
        pltpu.make_async_copy(zero_ref, out_ref.at[k], sem).start()
        return c

    lax.fori_loop(0, count_ref[0], send, 0)
    lax.fori_loop(count_ref[0], slots, blank, 0)

    pltpu.make_async_copy(out_ref, out_ref, sem).wait()


def finish_kernel(rep_ref, base_ref, own_ref, *refs):
    terms, quarters, (out_ref, grads_ref, held_ref) = refs[:5], refs[5:9], refs[9:]
    total = own_ref[...]
    for t in terms:
        total = total + t[...].astype(jnp.float32)
    out_ref[...] = (base_ref[...] + total.T).astype(jnp.bfloat16)
    for k, q in enumerate(quarters):
        held_ref[rep_ref[0] ^ k] = q[...]
    for i in range(2):
        grads_ref[i, :, :128] = held_ref[2 * i]
        grads_ref[i, :, 128:] = held_ref[2 * i + 1]


def shape(s, t=jnp.bfloat16):
    return jax.ShapeDtypeStruct(s, t)


def call(kernel, name, outs, ins, flops=0, moved=1 << 20, scratch=(), limit=24):
    return pl.pallas_call(
        kernel,
        out_shape=outs,
        in_specs=ins,
        out_specs=jax.tree.map(lambda _: VMEM, outs),
        scratch_shapes=scratch,
        compiler_params=pltpu.CompilerParams(vmem_limit_bytes=limit << 20),
        cost_estimate=pl.CostEstimate(flops=flops, bytes_accessed=moved, transcendentals=0),
        name=name,
    )


def local(node_feats, tile_vals, tile_row, tile_col, tile_count, w_agg, w_self, bias, cotangent):
    n_blk, n_rep = lax.axis_size("blk"), lax.axis_size("rep")
    group = lax.axis_index("blk")
    half, line = (group // 4) & 1, group & 3
    rep = lax.axis_index("rep").reshape(1).astype(jnp.int32)
    ring = group.reshape(1).astype(jnp.int32)
    count = tile_count[0]
    away = (lax.div(tile_col[0, 0], 2) - group + n_blk) & (n_blk - 1)
    place = jnp.zeros_like(away)
    for d in DISTANCES[1:]:
        place = place + (away >= d).astype(jnp.int32)
    swapped = (line >= 2) & ((away == 4) | (away == 60) | (away == 2) | (away == 62))
    place = jnp.where(swapped, 12 - place, place)
    at = (24 * tile_row[0, 0] + 2 * place + lax.rem(tile_col[0, 0], 2)).astype(jnp.int32)

    def move(x, source):
        pairs = [(source(g) * n_rep + r, g * n_rep + r) for g in range(n_blk) for r in range(n_rep)]
        return lax.ppermute(x, ("blk", "rep"), pairs)

    def from_blk(x, d):
        return move(x, lambda g: (g + d) % n_blk)

    def flip(x):
        return move(x, lambda g: g ^ 4)

    def from_plane(x, sign):
        return move(x, lambda g: (g + (8 * sign if g & 4 else -8 * sign)) % n_blk)

    def to_rep(x, k):
        return lax.ppermute(x, "rep", [(i, i ^ k) for i in range(n_rep)])

    def add(a, b):
        return (a.astype(jnp.float32) + b.astype(jnp.float32)).astype(jnp.bfloat16)

    def cross(g):
        return (g + 4 if g & 3 < 2 else g - 4) % n_blk

    def other(g):
        return (g - 4 if g & 3 < 2 else g + 4) % n_blk

    crossing = move(node_feats, cross)
    up, down = from_blk(node_feats, 8), from_blk(node_feats, -8)
    over2 = move(node_feats, lambda g: g ^ 2)
    up2, down2 = from_blk(up, 8), from_blk(down, -8)
    right = move(jnp.where(line == 0, crossing, node_feats), lambda g: g & ~3 | (g + 1) & 3)
    left = move(jnp.where(line == 3, crossing, node_feats), lambda g: g & ~3 | (g - 1) & 3)
    cross2 = move(crossing, lambda g: g ^ 2)
    rest = move(node_feats, other)
    up4 = from_blk(up2, 16)
    feats = [node_feats, right, over2, crossing, up, up2, up4, down2, down, rest, cross2, left]

    dense = call(
        build_kernel, "build", shape((1024, 3072)), [SMEM, SMEM, HBM], moved=10 << 20,
        scratch=[
            pltpu.VMEM((192, 128, 128), jnp.float32),
            pltpu.VMEM((128, 128, 128), jnp.bfloat16),
            pltpu.SemaphoreType.DMA((4,)),
        ],
        limit=36,
    )(at, count, pltpu.with_memory_space_constraint(tile_vals[0, 0], pltpu.HBM))

    block = (256, 256)
    work = 2 * 1024 * 3072 * 256

    def forward(ks, types):
        return call(
            functools.partial(forward_kernel, ks), "forward", [shape(block, t) for t in types],
            [SMEM, VMEM] + [VMEM] * 12, flops=work // 2, moved=4 << 20,
        )(rep, dense, *feats)

    near, far = forward((1, 3), (jnp.bfloat16, jnp.bfloat16))
    near, far = to_rep(near, 1), to_rep(far, 1)
    own, other = forward((0, 2), (jnp.float32, jnp.float32))
    far = to_rep(add(other, far), 2)

    quarter = shape((256, 128), jnp.float32)
    updated, dagg, base, g0, g1, g2, g3 = call(
        update_kernel, "update",
        [shape(block), shape(block), shape(block, jnp.float32)] + [quarter] * 4,
        [SMEM] + [VMEM] * 8, flops=12 * 256**3, moved=2 << 20,
        scratch=[pltpu.VMEM((4, 256, 128), jnp.float32)],
    )(rep, own, near, far, node_feats, cotangent, w_agg, w_self, bias.reshape(1, 256))

    def gather_rep(x):
        x2, x1 = to_rep(x, 2), to_rep(x, 1)
        return [x, x1, x2, to_rep(x2, 1)]

    daggs = gather_rep(dagg)
    terms = call(
        scatter_kernel, "scatter", [shape(block, jnp.float32)] + [shape(block)] * 11,
        [SMEM] * 2 + [VMEM] * 5, flops=work, moved=8 << 20,
    )(rep, ring, dense, *daggs)

    firsts = [from_blk(terms[7], 8), from_blk(terms[2], -1), from_blk(terms[10], 1), from_plane(terms[9], -1)]
    theirs = to_rep(g2 + to_rep(g3, 1), 2)
    mine = call(fold_kernel, "fold", quarter, [VMEM] * 3 + [ANY])(g0, to_rep(g1, 1), theirs, terms[0])
    pieces = lax.all_to_all(mine.reshape(n_blk, 4, 128), "blk", 0, 0, tiled=True)
    spread = call(spread_kernel, "spread", shape((n_blk, 4, 128), jnp.float32), [VMEM] + [ANY] * 4)(pieces, *firsts)
    def late(a, b):
        return call(late_sum_kernel, "late_sum", shape(block), [VMEM, VMEM, ANY])(a, b, spread)

    up2_sum = add(terms[5], from_blk(terms[6], -16))
    up_sum = late(terms[4], from_blk(up2_sum, -8))
    down_sum = late(terms[8], firsts[0])
    right_sum = late(terms[1], firsts[1])
    left_sum = late(terms[11], firsts[2])
    across_sum = late(terms[3], firsts[3])
    arrived = [
        from_blk(up_sum, -8), from_blk(down_sum, 8), from_blk(right_sum, -1), from_blk(left_sum, 1), flip(across_sum)
    ]

    tile_grads = pl.pallas_call(
        tile_grads_kernel,
        out_shape=shape((128, 128, 128)),
        in_specs=[SMEM] * 3 + [VMEM] * 16,
        out_specs=ANY,
        scratch_shapes=[
            pltpu.VMEM((192, 128, 128), jnp.bfloat16),
            pltpu.VMEM((1024, 256), jnp.bfloat16),
            pltpu.VMEM((128, 128), jnp.bfloat16),
            pltpu.SemaphoreType.DMA,
        ],
        compiler_params=pltpu.CompilerParams(vmem_limit_bytes=24 << 20),
        cost_estimate=pl.CostEstimate(flops=work, bytes_accessed=8 << 20, transcendentals=0),
        name="tile_grads",
    )(rep, at, count, *daggs, *feats)

    whole = lax.all_to_all(spread, "blk", 0, 0, tiled=True).reshape(256, 128)
    feat_grad, weight_grads = call(
        finish_kernel, "finish", [shape(block), shape((2, 256, 256), jnp.float32)], [SMEM] + [VMEM] * 11,
        scratch=[pltpu.VMEM((4, 256, 128), jnp.float32)],
    )(rep, base, terms[0], *arrived, *gather_rep(whole))
    return updated, feat_grad, tile_grads.reshape(1, 1, 128, 128, 128), weight_grads


def solution(mesh):
    in_specs = (
        P(("blk", "rep"), None),
        P("blk", "rep", None, None, None),
        P("blk", "rep", None),
        P("blk", "rep", None),
        P("blk", "rep"),
        P(),
        P(),
        P(),
        P(("blk", "rep"), None),
    )
    out_specs = (
        P(("blk", "rep"), None),
        P(("blk", "rep"), None),
        P("blk", "rep", None, None, None),
        P(),
    )
    return jax.shard_map(local, mesh=mesh, in_specs=in_specs, out_specs=out_specs, check_vma=False)
```
